32 devices in a mesh: parts: 1, blk: 32 (over z, y, x, core), col: 1.
Axes of the slice: x: 2, y: 2, z: 4, core: 2. Of those that a mesh axis runs over, the one named last changes fastest.
Arguments:
- activations: bfloat16 [8192, 28672], P(('parts', 'blk'), 'col'), may hold values from -6 to 6
- out_grads: bfloat16 [8192, 8192], P(('parts', 'blk'), 'col'), may hold values from -6 to 6
- input_basis: float32 [28672, 256], P(('parts', 'col', 'blk')), may hold values from -0.03125 to 0.03125
- output_basis: float32 [8192, 256], P(('parts', 'col', 'blk')), may hold values from -0.0625 to 0.0625
- query_rotated: bfloat16 [64, 256, 256], P('parts', None, 'col'), may hold values from -0.0234375 to 0.0234375
- eigenvalues: float32 [256, 256], P('parts', 'col'), may hold values from 0.3 to 3
Outputs:
- scores: float32 [64, 8192], P('parts', 'blk')
The draws below stay inside these ranges and needn't reach their ends.
All inputs are finite; a program needn't handle non-finite values.
Results may differ from the reference program's by a relative error of at most 0.0003.
Values sent between devices are 32-bit elements; how exact they have to be, the bound alone decides.
A program may use at most 128 MiB of HBM per device.

```python
import math
import jax
import jax.numpy as jnp
from jax import lax

FEAT_IN = 28672
FEAT_OUT = 8192
KEEP_IN = 256
KEEP_OUT = 256
QUERIES = 64
TOKENS = 8192


def block_levels(stream_key, dims, split, smallest, largest):
    factor_of, own = 1.0, jax.random.fold_in(stream_key, 6)
    for dim, blocks in split:
        heights = jnp.exp(jax.random.uniform(jax.random.fold_in(own, dim), (blocks,), jnp.float32, smallest / len(split), largest / len(split)))
        factor_of = factor_of * jnp.repeat(heights, dims[dim] // blocks).reshape([-1 if axis == dim else 1 for axis in range(len(dims))])
    return factor_of


def normal_values(own_key, dims, deviation, limit, pieces=(), kind=jnp.bfloat16):
    factor_of = block_levels(own_key, dims, pieces, -0.22, 0.18) if pieces else 1.0
    values = jax.random.normal(own_key, dims, jnp.float32) * deviation * factor_of
    return jnp.minimum(jnp.maximum(values, -limit), limit).astype(kind)


def setup_inputs(seed: int = 0, part: int = 0) -> dict:
    splits = jax.random.split(jax.random.key(seed), 7)
    part_keys = jax.random.split(jax.random.fold_in(splits[6], part), 7)
    return {
        "activations": normal_values(part_keys[0], (TOKENS, FEAT_IN), 1.0, 6.0, ((0, 32),)),
        "out_grads": normal_values(part_keys[1], (TOKENS, FEAT_OUT), 1.0, 6.0, ((0, 32),)),
        "input_basis": normal_values(part_keys[2], (FEAT_IN, KEEP_IN), FEAT_IN ** -0.5, 0.03125, ((0, 32),), jnp.float32),
        "output_basis": normal_values(part_keys[3], (FEAT_OUT, KEEP_OUT), FEAT_OUT ** -0.5, 0.0625, ((0, 32),), jnp.float32),
        "query_rotated": normal_values(part_keys[4], (QUERIES, KEEP_OUT, KEEP_IN), (KEEP_OUT * KEEP_IN) ** -0.5, 0.0234375),
        "eigenvalues": jnp.clip(jnp.exp(jax.random.uniform(part_keys[5], (KEEP_OUT, KEEP_IN), jnp.float32, math.log(0.3), math.log(3.0))), 0.3, 3.0),
    }


def reference(activations, out_grads, input_basis, output_basis, query_rotated, eigenvalues):
    highest = lax.Precision.HIGHEST
    rotated_in = jnp.dot(activations.astype(jnp.float32), input_basis, precision=highest, preferred_element_type=jnp.float32)
    rotated_out = jnp.dot(out_grads.astype(jnp.float32), output_basis, precision=highest, preferred_element_type=jnp.float32)
    scaled = query_rotated.astype(jnp.float32) / eigenvalues[None, :, :]

    def one_query(matrix):
        mixed = jnp.dot(rotated_in, matrix.T, precision=highest, preferred_element_type=jnp.float32)
        return jnp.sum(mixed * rotated_out, axis=1)

    return lax.map(one_query, scaled)
```

```python
import functools

import jax
import jax.numpy as jnp
from jax import lax
from jax.experimental import pallas as pl
from jax.experimental.pallas import tpu as pltpu
from jax.sharding import PartitionSpec as P

MESH = pl.DeviceIdType.MESH
F32, BF16 = jnp.float32, jnp.bfloat16
SLOTS = 5
LINKS = 4
PIECES_IN, PIECES_OUT = 8, 4
QUERY_STEP = 4

O, X, Y, D = 0, 1, 2, 3


def _table(text):
    pairs = (text[at : at + 2] for at in range(0, len(text), 2))
    return [None if e == "--" else ("OXYD".index(e[0]), int(e[1])) for e in pairs]


ARRIVE = (
    {0: _table("X0D0X1X2X3"), 1: _table("Y0Y1Y2D1Y3"), 2: _table("O1O2O3D2D3")},
    {
        0: _table("X1X2D1X0X3"),
        1: _table("Y1Y2D2Y0Y3"),
        2: _table("O2O3--D3--"),
        3: _table("O0--D0----"),
    },
)


def _sent(kind, link, slot):
    if link == 3:
        return ARRIVE[0][2][slot] if kind == 1 else None
    if link == 2:
        if kind == 0:
            return ARRIVE[1][3][slot]
        entry = ARRIVE[1][2][slot]
        return None if entry is None else (entry[0], 3 - entry[1])
    entry = ARRIVE[kind][link][slot]
    return entry[0] ^ (1, 2)[link], entry[1]


def _received(kind, link):
    if link == 3:
        return 2
    return 3 if link == 2 and kind == 0 else link


def _split(value):
    high = value.astype(BF16)
    return high, (value - high.astype(F32)).astype(BF16)


def _dot(a, b):
    return jnp.dot(a, b, preferred_element_type=F32)


def kernel(
    act, grads, basis_in, basis_out, query, eig, scores,
    all_in, all_out, mixed, grads_v, act_v, query_v, inverse, total_in, total_out, r_high, r_low,
    send_in, recv_in, sib_send_in, sib_recv_in, send_out, recv_out, sib_send_out, sib_recv_out,
    load_sem, act_sem, query_sem,
):
    me = lax.axis_index("blk")
    core, x, y, z = me % 2, (me // 2) % 2, (me // 4) % 2, me // 8
    flip = z // 2
    plane = z + flip * (3 - 2 * z)
    sibling = me + 1 - 2 * core
    inner = me + 8 - 16 * flip
    outer = me - 8 + 16 * flip
    target = (me + 2 - 4 * x, me + 4 - 8 * y, inner, outer)
    middle = plane == 1

    def device(column, from_plane, of_core):
        xx, yy = (x + column % 2) % 2, (y + column // 2) % 2
        zz = from_plane + flip * (3 - 2 * from_plane)
        return zz * 8 + yy * 4 + xx * 2 + of_core

    own = [
        pltpu.make_async_copy(basis_in, all_in.at[me], load_sem.at[0]),
        pltpu.make_async_copy(basis_out, all_out.at[me], load_sem.at[1]),
        pltpu.make_async_copy(grads, grads_v, load_sem.at[2]),
    ]
    for copy in own:
        copy.start()

    barrier = pltpu.get_barrier_semaphore()
    for other in (sibling, target[0], target[1], inner):
        pl.semaphore_signal(barrier, inc=1, device_id={"blk": other}, device_id_type=MESH)

    @pl.when(middle)
    def _():
        pl.semaphore_signal(barrier, inc=1, device_id={"blk": outer}, device_id_type=MESH)
        pl.semaphore_wait(barrier, 5)

    @pl.when(jnp.logical_not(middle))
    def _():
        pl.semaphore_wait(barrier, 4)

    inverse[...] = 1.0 / eig[...]
    total_in[...] = jnp.zeros_like(total_in)
    total_out[...] = jnp.zeros_like(total_out)

    class Phase:
        def __init__(self, held, pieces, send, recv, sib_send, sib_recv):
            self.held, self.pieces = held, pieces
            self.send, self.recv, self.sib_send, self.sib_recv = send, recv, sib_send, sib_recv
            self.rows = held.shape[1] // pieces

        def part(self, index, p):
            return self.held.at[index, pl.ds(pl.multiple_of(p * self.rows, 8), self.rows)]

        def link_copy(self, entry, link, slot, p, there=None):
            ref = self.part(device(*entry, core), p)
            there = link if there is None else there
            return pltpu.make_async_remote_copy(
                src_ref=ref, dst_ref=ref, send_sem=self.send.at[link, slot, p],
                recv_sem=self.recv.at[there, slot, p], device_id={"blk": target[link]}, device_id_type=MESH,
            )

        def sib_copy(self, index, link, slot, p):
            ref = self.part(index, p)
            return pltpu.make_async_remote_copy(
                src_ref=ref, dst_ref=ref, send_sem=self.sib_send.at[link, slot, p],
                recv_sem=self.sib_recv.at[link, slot, p], device_id={"blk": sibling}, device_id_type=MESH,
            )

        def both(self, body):
            for kind in (0, 1):
                pl.when(plane == kind)(functools.partial(body, kind))

        def send_slot(self, kind, slot, p):
            for link in range(LINKS):
                entry = _sent(kind, link, slot)
                if entry is not None:
                    self.link_copy(entry, link, slot, p, _received(kind, link)).start()

        def begin(self):
            @pl.loop(0, self.pieces)
            def _(p):
                self.both(lambda kind: self.send_slot(kind, 0, p))
                self.sib_copy(me, LINKS, 0, p).start()

        def step(self, slot, p):
            def body(kind):
                for link, entries in ARRIVE[kind].items():
                    if entries[slot] is not None:
                        self.link_copy(entries[slot], link, slot, p).wait_recv()
                if slot + 1 < SLOTS:
                    self.send_slot(kind, slot + 1, p)
                for link, entries in ARRIVE[kind].items():
                    if entries[slot] is not None:
                        self.sib_copy(device(*entries[slot], core), link, slot, p).start()

            self.both(body)

        def unit(self, slot, n):
            link = n % LINKS
            code = jnp.int32(-1)
            for at in range(LINKS):
                ends = [ARRIVE[kind].get(at, [None] * SLOTS)[slot] for kind in (0, 1)]
                ends = [-1 if e is None else e[0] + 4 * e[1] for e in ends]
                code = jnp.where(link == at, jnp.where(middle, ends[1], ends[0]), code)
            from_core = core + (n // LINKS) * (1 - 2 * core)
            some = jnp.maximum(code, 0)
            return code >= 0, device(some % 4, some // 4, from_core), link

        def wait_sibling(self, index, link, slot):
            @pl.loop(0, self.pieces)
            def _(p):
                self.sib_copy(index, link, slot, p).wait_recv()

        def drain(self):
            @pl.loop(0, self.pieces)
            def _(p):
                def body(kind):
                    for slot in range(SLOTS):
                        for link in range(LINKS):
                            entry = _sent(kind, link, slot)
                            if entry is not None:
                                self.link_copy(entry, link, slot, p).wait_send()
                        for link, entries in ARRIVE[kind].items():
                            if entries[slot] is not None:
                                self.sib_copy(device(*entries[slot], core), link, slot, p).wait_send()

                self.both(body)
                self.sib_copy(me, LINKS, 0, p).wait_send()

    first = Phase(all_in, PIECES_IN, send_in, recv_in, sib_send_in, sib_recv_in)
    second = Phase(all_out, PIECES_OUT, send_out, recv_out, sib_send_out, sib_recv_out)
    depth_in, depth_out = all_in.shape[1], all_out.shape[1]

    def act_copy(index):
        columns = pl.ds(pl.multiple_of(index * depth_in, 128), depth_in)
        return pltpu.make_async_copy(act.at[:, columns], act_v, act_sem)

    def add_in(index):
        high, low = _split(all_in[index])
        block = act_v[...]
        total_in[...] += _dot(block, high) + _dot(block, low)

    def add_out(index):
        high, low = _split(all_out[index])
        block = grads_v[:, pl.ds(pl.multiple_of(index * depth_out, 128), depth_out)]
        total_out[...] += _dot(block, high) + _dot(block, low)

    def unit_in(slot, n, between):
        valid, index, link = first.unit(slot, n)
        pl.when(valid)(lambda: act_copy(index).start())
        between()

        @pl.when(valid)
        def _():
            pl.when(n >= LINKS)(lambda: first.wait_sibling(index, link, slot))
            act_copy(index).wait()
            add_in(index)

    def unit_out(slot, n):
        valid, index, link = second.unit(slot, n)

        @pl.when(valid)
        def _():
            pl.when(n >= LINKS)(lambda: second.wait_sibling(index, link, slot))
            add_out(index)

    def query_copy(chunk, at):
        rows = pl.ds(chunk * QUERY_STEP, QUERY_STEP)
        return pltpu.make_async_copy(query.at[rows], query_v.at[at], query_sem.at[at])

    own[0].wait()
    first.begin()

    @pl.loop(0, PIECES_IN)
    def _(p):
        index = me + (p % 2) * (sibling - me)
        pl.when(p < 2)(lambda: act_copy(index).start())
        first.step(0, p)

        @pl.when(p < 2)
        def _():
            pl.when(p == 1)(lambda: first.wait_sibling(sibling, LINKS, 0))
            act_copy(index).wait()
            add_in(index)

    for slot in range(1, SLOTS):
        if slot == SLOTS - 1:
            own[1].wait()
            own[2].wait()
            second.begin()

        @pl.loop(0, PIECES_IN)
        def _(p, slot=slot):
            unit_in(slot - 1, p, lambda: first.step(slot, p))

    per_step = 2 * LINKS // PIECES_OUT

    @pl.loop(0, PIECES_OUT)
    def _(p):
        @pl.loop(0, per_step)
        def _(k):
            def between():
                pl.when(k == 0)(lambda: second.step(0, p))

            unit_in(SLOTS - 1, p * per_step + k, between)

    second.wait_sibling(sibling, LINKS, 0)
    add_out(me)
    add_out(sibling)
    high, low = _split(total_in[...].T)
    r_high[...] = high
    r_low[...] = low
    query_copy(0, 0).start()

    chunks = query.shape[0] // QUERY_STEP
    per_slot = chunks // (SLOTS - 1)
    chunks_step = per_slot // PIECES_OUT
    keep = query.shape[1]
    for slot in range(1, SLOTS):

        @pl.loop(0, PIECES_OUT)
        def _(p, slot=slot):
            second.step(slot, p)

            @pl.loop(0, per_step)
            def _(k):
                unit_out(slot - 1, p * per_step + k)

            @pl.loop(0, chunks_step)
            def _(k):
                chunk = (slot - 1) * per_slot + p * chunks_step + k
                at = chunk % 2
                pl.when(chunk + 1 < chunks)(lambda: query_copy(chunk + 1, 1 - at).start())
                query_copy(chunk, at).wait()
                scaled = query_v[at].astype(F32) * inverse[...][None]
                s_high, s_low = _split(scaled.reshape(QUERY_STEP * keep, -1))
                value = _dot(s_high, r_high[...]) + (_dot(s_high, r_low[...]) + _dot(s_low, r_high[...]))
                mixed[pl.ds(chunk * QUERY_STEP, QUERY_STEP)] = value.reshape(QUERY_STEP, keep, -1)

    @pl.loop(0, 2 * LINKS)
    def _(n):
        unit_out(SLOTS - 1, n)

    turned = total_out[...].T

    @pl.loop(0, query.shape[0] // 8)
    def _(b):
        rows = pl.ds(pl.multiple_of(b * 8, 8), 8)
        scores[rows, :] = jnp.sum(mixed[rows] * turned[None], axis=1)

    first.drain()
    second.drain()


def gathered(activations, out_grads, input_basis, output_basis, query_rotated, eigenvalues):
    blocks = lax.axis_size("blk")
    tokens = activations.shape[0]
    queries, keep_out, keep_in = query_rotated.shape
    any_space = pl.BlockSpec(memory_space=pl.ANY)
    vmem = pl.BlockSpec(memory_space=pltpu.VMEM)

    def sems(pieces):
        dma = pltpu.SemaphoreType.DMA
        return [
            dma((LINKS, SLOTS, pieces)),
            dma((LINKS, SLOTS, pieces)),
            dma((LINKS + 1, SLOTS, pieces)),
            dma((LINKS + 1, SLOTS, pieces)),
        ]

    macs = tokens * (activations.shape[1] * keep_in + out_grads.shape[1] * keep_out)
    macs += tokens * queries * keep_out * keep_in
    return pl.pallas_call(
        kernel,
        out_shape=jax.ShapeDtypeStruct((queries, tokens), F32),
        in_specs=[any_space] * 5 + [vmem],
        out_specs=vmem,
        scratch_shapes=[
            pltpu.VMEM((blocks, *input_basis.shape), F32),
            pltpu.VMEM((blocks, *output_basis.shape), F32),
            pltpu.VMEM((queries, keep_out, tokens), F32),
            pltpu.VMEM(out_grads.shape, BF16),
            pltpu.VMEM((tokens, input_basis.shape[0]), BF16),
            pltpu.VMEM((2, QUERY_STEP, keep_out, keep_in), BF16),
            pltpu.VMEM((keep_out, keep_in), F32),
            pltpu.VMEM((tokens, keep_in), F32),
            pltpu.VMEM((tokens, keep_out), F32),
            pltpu.VMEM((keep_in, tokens), BF16),
            pltpu.VMEM((keep_in, tokens), BF16),
            *sems(PIECES_IN),
            *sems(PIECES_OUT),
            pltpu.SemaphoreType.DMA((3,)),
            pltpu.SemaphoreType.DMA,
            pltpu.SemaphoreType.DMA((2,)),
        ],
        cost_estimate=pl.CostEstimate(flops=2 * macs, bytes_accessed=1 << 25, transcendentals=0),
        compiler_params=pltpu.CompilerParams(
            collective_id=0, has_side_effects=True, vmem_limit_bytes=63 << 20
        ),
    )(activations, out_grads, input_basis, output_basis, query_rotated, eigenvalues)


def per_device(activations, out_grads, input_basis, output_basis, query_rotated, eigenvalues):
    highest = lax.Precision.HIGHEST
    block = out_grads.astype(jnp.float32)
    out_part = jnp.dot(
        block,
        lax.all_gather(output_basis, "blk", axis=0, tiled=True),
        precision=highest,
        preferred_element_type=jnp.float32,
    )
    block = activations.astype(jnp.float32)
    in_part = jnp.dot(
        block,
        lax.all_gather(input_basis, "blk", axis=0, tiled=True),
        precision=highest,
        preferred_element_type=jnp.float32,
    )
    rotated_in = lax.psum_scatter(in_part, "col", scatter_dimension=1, tiled=True)
    rotated_out = lax.psum(out_part, "col")
    scaled = query_rotated.astype(jnp.float32) / eigenvalues[None, :, :]
    mixed = jnp.einsum(
        "qij,tj->qit", scaled, rotated_in, precision=highest, preferred_element_type=jnp.float32
    )
    partial_scores = jnp.einsum(
        "qit,ti->qt", mixed, rotated_out, precision=highest, preferred_element_type=jnp.float32
    )
    return lax.psum(partial_scores, "col")


def solution(mesh):
    shape = dict(mesh.shape)
    routed = shape["blk"] == 32 and shape["parts"] == 1 and shape["col"] == 1
    return jax.shard_map(
        gathered if routed else per_device,
        mesh=mesh,
        in_specs=(
            P(("parts", "blk"), "col"),
            P(("parts", "blk"), "col"),
            P(("parts", "col", "blk"), None),
            P(("parts", "col", "blk"), None),
            P("parts", None, "col"),
            P("parts", "col"),
        ),
        out_specs=P("parts", "blk"),
        check_vma=False,
    )
```

```python
import functools

import jax
import jax.numpy as jnp
from jax import lax
from jax.experimental import pallas as pl
from jax.experimental.pallas import tpu as pltpu
from jax.sharding import PartitionSpec as P

MESH = pl.DeviceIdType.MESH
F32, BF16 = jnp.float32, jnp.bfloat16
SLOTS = 5
LINKS = 4
ROWS_IN, ROWS_OUT = 256, 128
UNITS = 2 * LINKS
QUERY_STEP = 4

O, X, Y, D = 0, 1, 2, 3


def _table(text):
    pairs = (text[at : at + 2] for at in range(0, len(text), 2))
    return [None if e == "--" else ("OXYD".index(e[0]), int(e[1])) for e in pairs]


ARRIVE = (
    {0: _table("X0D0X1X2X3"), 1: _table("Y0Y1Y2D1Y3"), 2: _table("O1O2O3D2D3")},
    {
        0: _table("X1X2D1X0X3"),
        1: _table("Y1Y2D2Y0Y3"),
        2: _table("O2O3--D3--"),
        3: _table("O0--D0----"),
    },
)


def _sent(kind, link, slot):
    if link == 3:
        return ARRIVE[0][2][slot] if kind == 1 else None
    if link == 2:
        if kind == 0:
            return ARRIVE[1][3][slot]
        entry = ARRIVE[1][2][slot]
        return None if entry is None else (entry[0], 3 - entry[1])
    entry = ARRIVE[kind][link][slot]
    return entry[0] ^ (1, 2)[link], entry[1]


def _received(kind, link):
    if link == 3:
        return 2
    return 3 if link == 2 and kind == 0 else link


def _split(value):
    high = value.astype(BF16)
    return high, (value - high.astype(F32)).astype(BF16)


def _dot(a, b):
    return jnp.dot(a, b, preferred_element_type=F32)


def kernel(
    act, grads, basis_in, basis_out, query, eig, scores,
    all_in, all_out, mixed, grads_v, act_v, query_v, inverse, total_in, total_out, r_high, r_low,
    send_in, recv_in, sib_send_in, sib_recv_in, send_out, recv_out, sib_send_out, sib_recv_out,
    load_sem, act_sem, query_sem, last_sem,
):
    me = lax.axis_index("blk")
    core, x, y, z = me % 2, (me // 2) % 2, (me // 4) % 2, me // 8
    flip = z // 2
    plane = z + flip * (3 - 2 * z)
    sibling = me + 1 - 2 * core
    inner = me + 8 - 16 * flip
    outer = me - 8 + 16 * flip
    target = (me + 2 - 4 * x, me + 4 - 8 * y, inner, outer)
    middle = plane == 1

    def device(column, from_plane, of_core):
        xx, yy = (x + column % 2) % 2, (y + column // 2) % 2
        zz = from_plane + flip * (3 - 2 * from_plane)
        return zz * 8 + yy * 4 + xx * 2 + of_core

    own = [
        pltpu.make_async_copy(basis_in, all_in.at[me], load_sem.at[0]),
        pltpu.make_async_copy(basis_out, all_out.at[me], load_sem.at[1]),
        pltpu.make_async_copy(grads, grads_v, load_sem.at[2]),
    ]
    for copy in own:
        copy.start()

    barrier = pltpu.get_barrier_semaphore()
    for other in (sibling, target[0], target[1], inner):
        pl.semaphore_signal(barrier, inc=1, device_id={"blk": other}, device_id_type=MESH)

    @pl.when(middle)
    def _():
        pl.semaphore_signal(barrier, inc=1, device_id={"blk": outer}, device_id_type=MESH)
        pl.semaphore_wait(barrier, 5)

    @pl.when(jnp.logical_not(middle))
    def _():
        pl.semaphore_wait(barrier, 4)

    inverse[...] = 1.0 / eig[...]
    total_in[...] = jnp.zeros_like(total_in)
    total_out[...] = jnp.zeros_like(total_out)

    class Phase:
        def __init__(self, held, rows, send, recv, sib_send, sib_recv):
            self.held, self.rows = held, rows
            self.pieces = pl.cdiv(held.shape[1], rows)
            self.whole = held.shape[1] // rows
            self.every = UNITS // self.pieces
            self.send, self.recv, self.sib_send, self.sib_recv = send, recv, sib_send, sib_recv

        def length(self, p):
            return self.held.shape[1] % self.rows if isinstance(p, int) and p == self.whole else self.rows

        def each(self, body):
            pl.loop(0, self.whole)(body)
            if self.whole < self.pieces:
                body(self.whole)

        def at(self, n, body, lag=0):
            n = n - lag
            whole = jnp.logical_and(n % self.every == 0, n < self.whole * self.every)
            pl.when(jnp.logical_and(whole, n >= 0))(lambda: body(n // self.every))
            if self.whole < self.pieces:
                pl.when(n == self.whole * self.every)(lambda: body(self.whole))

        def part(self, index, p):
            return self.held.at[index, pl.ds(pl.multiple_of(p * self.rows, 128), self.length(p))]

        def link_copy(self, entry, link, slot, p, there=None):
            ref = self.part(device(*entry, core), p)
            there = link if there is None else there
            return pltpu.make_async_remote_copy(
                src_ref=ref, dst_ref=ref, send_sem=self.send.at[link, slot, p],
                recv_sem=self.recv.at[there, slot, p], device_id={"blk": target[link]}, device_id_type=MESH,
            )

        def sib_copy(self, index, link, slot, p):
            ref = self.part(index, p)
            return pltpu.make_async_remote_copy(
                src_ref=ref, dst_ref=ref, send_sem=self.sib_send.at[link, slot, p],
                recv_sem=self.sib_recv.at[link, slot, p], device_id={"blk": sibling}, device_id_type=MESH,
            )

        def both(self, body):
            for kind in (0, 1):
                pl.when(plane == kind)(functools.partial(body, kind))

        def send_slot(self, kind, slot, p):
            for link in range(LINKS):
                entry = _sent(kind, link, slot)
                if entry is not None:
                    self.link_copy(entry, link, slot, p, _received(kind, link)).start()

        def begin(self):
            @self.each
            def _(p):
                self.both(lambda kind: self.send_slot(kind, 0, p))
                self.sib_copy(me, LINKS, 0, p).start()

        def step(self, slot, p):
            def body(kind):
                for link, entries in ARRIVE[kind].items():
                    if entries[slot] is not None:
                        self.link_copy(entries[slot], link, slot, p).wait_recv()
                if slot + 1 < SLOTS:
                    self.send_slot(kind, slot + 1, p)
                for link, entries in ARRIVE[kind].items():
                    if entries[slot] is not None:
                        self.sib_copy(device(*entries[slot], core), link, slot, p).start()

            self.both(body)

        def unit(self, slot, n):
            link = n % LINKS
            code = jnp.int32(-1)
            for at in range(LINKS):
                ends = [ARRIVE[kind].get(at, [None] * SLOTS)[slot] for kind in (0, 1)]
                ends = [-1 if e is None else e[0] + 4 * e[1] for e in ends]
                code = jnp.where(link == at, jnp.where(middle, ends[1], ends[0]), code)
            from_core = core + (n // LINKS) * (1 - 2 * core)
            some = jnp.maximum(code, 0)
            return code >= 0, device(some % 4, some // 4, from_core), link

        def wait_sibling(self, index, link, slot):
            @self.each
            def _(p):
                self.sib_copy(index, link, slot, p).wait_recv()

        def drain(self):
            @self.each
            def _(p):
                def body(kind):
                    for slot in range(SLOTS):
                        for link in range(LINKS):
                            entry = _sent(kind, link, slot)
                            if entry is not None:
                                self.link_copy(entry, link, slot, p).wait_send()
                        for link, entries in ARRIVE[kind].items():
                            if entries[slot] is not None:
                                self.sib_copy(device(*entries[slot], core), link, slot, p).wait_send()

                self.both(body)
                self.sib_copy(me, LINKS, 0, p).wait_send()

    first = Phase(all_in, ROWS_IN, send_in, recv_in, sib_send_in, sib_recv_in)
    second = Phase(all_out, ROWS_OUT, send_out, recv_out, sib_send_out, sib_recv_out)
    depth_in, depth_out = all_in.shape[1], all_out.shape[1]

    def act_copy(index):
        columns = pl.ds(pl.multiple_of(index * depth_in, 128), depth_in)
        return pltpu.make_async_copy(act.at[:, columns], act_v, act_sem)

    def add_in(index):
        high, low = _split(all_in[index])
        block = act_v[...]
        total_in[...] += _dot(block, high) + _dot(block, low)

    def add_out(index):
        high, low = _split(all_out[index])
        block = grads_v[:, pl.ds(pl.multiple_of(index * depth_out, 128), depth_out)]
        total_out[...] += _dot(block, high) + _dot(block, low)

    def unit_in(slot, n, between):
        valid, index, link = first.unit(slot, n)
        pl.when(valid)(lambda: act_copy(index).start())
        between()

        @pl.when(valid)
        def _():
            pl.when(n >= LINKS)(lambda: first.wait_sibling(index, link, slot))
            act_copy(index).wait()
            add_in(index)

    def unit_out(slot, n):
        valid, index, link = second.unit(slot, n)

        @pl.when(valid)
        def _():
            pl.when(n >= LINKS)(lambda: second.wait_sibling(index, link, slot))
            add_out(index)

    def query_copy(chunk, at):
        rows = pl.ds(chunk * QUERY_STEP, QUERY_STEP)
        return pltpu.make_async_copy(query.at[rows], query_v.at[at], query_sem.at[at])

    own[1].wait()
    second.begin()
    own[2].wait()

    @pl.loop(0, UNITS)
    def _(n):
        second.at(n, lambda p: second.step(0, p))
        pl.when(n == 0)(lambda: add_out(me))

    second.wait_sibling(sibling, LINKS, 0)
    add_out(sibling)
    for slot in range(1, SLOTS):
        if slot == SLOTS - 1:
            own[0].wait()
            first.begin()

        @pl.loop(0, UNITS)
        def _(n, slot=slot):
            second.at(n, lambda p: second.step(slot, p))
            unit_out(slot - 1, n)

    query_copy(0, 0).start()

    @pl.loop(0, UNITS)
    def _(n):
        index = me + (n % 2) * (sibling - me)
        pl.when(n < 2)(lambda: act_copy(index).start())
        first.at(n, lambda p: first.step(0, p))

        @pl.when(n < 2)
        def _():
            pl.when(n == 1)(lambda: first.wait_sibling(sibling, LINKS, 0))
            act_copy(index).wait()
            add_in(index)

        @pl.when(n == 3)
        def _():
            @pl.loop(0, UNITS)
            def _(k):
                unit_out(SLOTS - 1, k)

            high, low = _split(total_out[...].T)
            r_high[...] = high
            r_low[...] = low

    chunks = query.shape[0] // QUERY_STEP

    def mix(chunk):
        at = chunk % 2
        pl.when(chunk + 1 < chunks)(lambda: query_copy(chunk + 1, 1 - at).start())
        query_copy(chunk, at).wait()
        for k in range(QUERY_STEP):
            scaled = (query_v[at, k].astype(F32) * inverse[...]).T
            s_high, s_low = _split(scaled)
            value = _dot(s_high, r_high[...]) + (_dot(s_high, r_low[...]) + _dot(s_low, r_high[...]))
            mixed[chunk * QUERY_STEP + k] = value

    def last_copy(n, index):
        source = pl.ds(pl.multiple_of(index * depth_in, 128), depth_in)
        columns = pl.ds(pl.multiple_of(n * depth_in, 128), depth_in)
        return pltpu.make_async_copy(act.at[:, source], grads_v.at[:, columns], last_sem.at[n])

    def add_piece(n, index, p):
        rows = first.length(p)
        high, low = _split(all_in[index, pl.ds(pl.multiple_of(p * first.rows, 128), rows)])
        block = grads_v[:, pl.ds(pl.multiple_of(n * depth_in + p * first.rows, 128), rows)]
        total_in[...] += _dot(block, high) + _dot(block, low)

    per_mix = pl.cdiv(chunks, (SLOTS - 2) * UNITS)
    for slot in range(1, SLOTS - 1):

        @pl.loop(0, UNITS)
        def _(n, slot=slot):
            unit_in(slot - 1, n, lambda: first.at(n, lambda p: first.step(slot, p)))
            for k in range(per_mix):
                chunk = ((slot - 1) * UNITS + n) * per_mix + k
                pl.when(chunk < chunks)(functools.partial(mix, chunk))

    last = SLOTS - 1

    @pl.loop(0, UNITS)
    def _(n):
        valid, index, _ = first.unit(last, n)
        pl.when(valid)(lambda: last_copy(n, index).start())

    @pl.loop(0, UNITS)
    def _(n):
        valid, index, _ = first.unit(last, n)
        pl.when(valid)(lambda: last_copy(n, index).wait())

    def pieces_of(base, p):
        @pl.loop(0, LINKS)
        def _(link):
            valid, index, _ = first.unit(last, base + link)

            @pl.when(valid)
            def _():
                if base:
                    first.sib_copy(index, link, last, p).wait_recv()
                add_piece(base + link, index, p)

    @pl.loop(0, UNITS)
    def _(n):
        unit_in(last - 1, n, lambda: first.at(n, lambda p: first.step(last, p)))
        first.at(n, lambda p: pieces_of(0, p))
        first.at(n, lambda p: pieces_of(LINKS, p), lag=1)

    turned = total_in[...].T

    @pl.loop(0, query.shape[0] // 8)
    def _(b):
        rows = pl.ds(pl.multiple_of(b * 8, 8), 8)
        scores[rows, :] = jnp.sum(mixed[rows] * turned[None], axis=1)

    first.drain()
    second.drain()


def gathered(activations, out_grads, input_basis, output_basis, query_rotated, eigenvalues):
    blocks = lax.axis_size("blk")
    tokens = activations.shape[0]
    queries, keep_out, keep_in = query_rotated.shape
    any_space = pl.BlockSpec(memory_space=pl.ANY)
    vmem = pl.BlockSpec(memory_space=pltpu.VMEM)

    def sems(pieces):
        dma = pltpu.SemaphoreType.DMA
        return [
            dma((LINKS, SLOTS, pieces)),
            dma((LINKS, SLOTS, pieces)),
            dma((LINKS + 1, SLOTS, pieces)),
            dma((LINKS + 1, SLOTS, pieces)),
        ]

    macs = tokens * (activations.shape[1] * keep_in + out_grads.shape[1] * keep_out)
    macs += tokens * queries * keep_out * keep_in
    return pl.pallas_call(
        kernel,
        out_shape=jax.ShapeDtypeStruct((queries, tokens), F32),
        in_specs=[any_space] * 5 + [vmem],
        out_specs=vmem,
        scratch_shapes=[
            pltpu.VMEM((blocks, *input_basis.shape), F32),
            pltpu.VMEM((blocks, *output_basis.shape), F32),
            pltpu.VMEM((queries, keep_in, tokens), F32),
            pltpu.VMEM(out_grads.shape, BF16),
            pltpu.VMEM((tokens, input_basis.shape[0]), BF16),
            pltpu.VMEM((2, QUERY_STEP, keep_out, keep_in), BF16),
            pltpu.VMEM((keep_out, keep_in), F32),
            pltpu.VMEM((tokens, keep_in), F32),
            pltpu.VMEM((tokens, keep_out), F32),
            pltpu.VMEM((keep_out, tokens), BF16),
            pltpu.VMEM((keep_out, tokens), BF16),
            *sems(pl.cdiv(input_basis.shape[0], ROWS_IN)),
            *sems(pl.cdiv(output_basis.shape[0], ROWS_OUT)),
            pltpu.SemaphoreType.DMA((3,)),
            pltpu.SemaphoreType.DMA,
            pltpu.SemaphoreType.DMA((2,)),
            pltpu.SemaphoreType.DMA((2 * LINKS,)),
        ],
        cost_estimate=pl.CostEstimate(flops=2 * macs, bytes_accessed=1 << 25, transcendentals=0),
        compiler_params=pltpu.CompilerParams(
            collective_id=0, has_side_effects=True, vmem_limit_bytes=63 << 20
        ),
    )(activations, out_grads, input_basis, output_basis, query_rotated, eigenvalues)


def per_device(activations, out_grads, input_basis, output_basis, query_rotated, eigenvalues):
    highest = lax.Precision.HIGHEST
    block = out_grads.astype(jnp.float32)
    out_part = jnp.dot(
        block,
        lax.all_gather(output_basis, "blk", axis=0, tiled=True),
        precision=highest,
        preferred_element_type=jnp.float32,
    )
    block = activations.astype(jnp.float32)
    in_part = jnp.dot(
        block,
        lax.all_gather(input_basis, "blk", axis=0, tiled=True),
        precision=highest,
        preferred_element_type=jnp.float32,
    )
    rotated_in = lax.psum_scatter(in_part, "col", scatter_dimension=1, tiled=True)
    rotated_out = lax.psum(out_part, "col")
    scaled = query_rotated.astype(jnp.float32) / eigenvalues[None, :, :]
    mixed = jnp.einsum(
        "qij,tj->qit", scaled, rotated_in, precision=highest, preferred_element_type=jnp.float32
    )
    partial_scores = jnp.einsum(
        "qit,ti->qt", mixed, rotated_out, precision=highest, preferred_element_type=jnp.float32
    )
    return lax.psum(partial_scores, "col")


def solution(mesh):
    shape = dict(mesh.shape)
    routed = shape["blk"] == 32 and shape["parts"] == 1 and shape["col"] == 1
    return jax.shard_map(
        gathered if routed else per_device,
        mesh=mesh,
        in_specs=(
            P(("parts", "blk"), "col"),
            P(("parts", "blk"), "col"),
            P(("parts", "col", "blk"), None),
            P(("parts", "col", "blk"), None),
            P("parts", None, "col"),
            P("parts", "col"),
        ),
        out_specs=P("parts", "blk"),
        check_vma=False,
    )
```

```python
import functools

import jax
import jax.numpy as jnp
from jax import lax
from jax.experimental import pallas as pl
from jax.experimental.pallas import tpu as pltpu
from jax.sharding import PartitionSpec as P

MESH = pl.DeviceIdType.MESH
F32, BF16 = jnp.float32, jnp.bfloat16
SLOTS = 5
LINKS = 4
ROWS_IN, ROWS_OUT = 256, 128
UNITS = 2 * LINKS
QUERY_STEP = 4

O, X, Y, D = 0, 1, 2, 3


def _table(text):
    pairs = (text[at : at + 2] for at in range(0, len(text), 2))
    return [None if e == "--" else ("OXYD".index(e[0]), int(e[1])) for e in pairs]


ARRIVE = (
    {0: _table("X0D0X1X2X3"), 1: _table("Y0Y1Y2D1Y3"), 2: _table("O1O2O3D2D3")},
    {
        0: _table("X1X2D1X0X3"),
        1: _table("Y1Y2D2Y0Y3"),
        2: _table("O2O3--D3--"),
        3: _table("O0--D0----"),
    },
)


def _sent(kind, link, slot):
    if link == 3:
        return ARRIVE[0][2][slot] if kind == 1 else None
    if link == 2:
        if kind == 0:
            return ARRIVE[1][3][slot]
        entry = ARRIVE[1][2][slot]
        return None if entry is None else (entry[0], 3 - entry[1])
    entry = ARRIVE[kind][link][slot]
    return entry[0] ^ (1, 2)[link], entry[1]


def _received(kind, link):
    if link == 3:
        return 2
    return 3 if link == 2 and kind == 0 else link


def _split(value):
    high = value.astype(BF16)
    return high, (value - high.astype(F32)).astype(BF16)


def _dot(a, b):
    return jnp.dot(a, b, preferred_element_type=F32)


def kernel(
    act, grads, basis_in, basis_out, query, eig, scores,
    all_in, all_out, mixed, grads_v, act_v, query_v, inverse, total_in, total_out, r_high, r_low,
    send_in, recv_in, sib_send_in, sib_recv_in, send_out, recv_out, sib_send_out, sib_recv_out,
    load_sem, act_sem, query_sem, last_sem,
):
    me = lax.axis_index("blk")
    core, x, y, z = me % 2, (me // 2) % 2, (me // 4) % 2, me // 8
    flip = z // 2
    plane = z + flip * (3 - 2 * z)
    sibling = me + 1 - 2 * core
    inner = me + 8 - 16 * flip
    outer = me - 8 + 16 * flip
    target = (me + 2 - 4 * x, me + 4 - 8 * y, inner, outer)
    middle = plane == 1

    def device(column, from_plane, of_core):
        xx, yy = (x + column % 2) % 2, (y + column // 2) % 2
        zz = from_plane + flip * (3 - 2 * from_plane)
        return zz * 8 + yy * 4 + xx * 2 + of_core

    own = [
        pltpu.make_async_copy(basis_in, all_in.at[me], load_sem.at[0]),
        pltpu.make_async_copy(basis_out, all_out.at[me], load_sem.at[1]),
        pltpu.make_async_copy(grads, grads_v, load_sem.at[2]),
    ]
    for copy in own:
        copy.start()

    barrier = pltpu.get_barrier_semaphore()
    for other in (sibling, target[0], target[1], inner):
        pl.semaphore_signal(barrier, inc=1, device_id={"blk": other}, device_id_type=MESH)

    @pl.when(middle)
    def _():
        pl.semaphore_signal(barrier, inc=1, device_id={"blk": outer}, device_id_type=MESH)
        pl.semaphore_wait(barrier, 5)

    @pl.when(jnp.logical_not(middle))
    def _():
        pl.semaphore_wait(barrier, 4)

    inverse[...] = 1.0 / eig[...]
    total_in[...] = jnp.zeros_like(total_in)
    total_out[...] = jnp.zeros_like(total_out)

    class Phase:
        def __init__(self, held, rows, send, recv, sib_send, sib_recv):
            self.held, self.rows = held, rows
            self.pieces = pl.cdiv(held.shape[1], rows)
            self.whole = held.shape[1] // rows
            self.every = UNITS // self.pieces
            self.send, self.recv, self.sib_send, self.sib_recv = send, recv, sib_send, sib_recv

        def length(self, p):
            return self.held.shape[1] % self.rows if isinstance(p, int) and p == self.whole else self.rows

        def each(self, body):
            pl.loop(0, self.whole)(body)
            if self.whole < self.pieces:
                body(self.whole)

        def at(self, n, body, lag=0):
            n = n - lag
            whole = jnp.logical_and(n % self.every == 0, n < self.whole * self.every)
            pl.when(jnp.logical_and(whole, n >= 0))(lambda: body(n // self.every))
            if self.whole < self.pieces:
                pl.when(n == self.whole * self.every)(lambda: body(self.whole))

        def part(self, index, p):
            return self.held.at[index, pl.ds(pl.multiple_of(p * self.rows, 128), self.length(p))]

        def link_copy(self, entry, link, slot, p, there=None):
            ref = self.part(device(*entry, core), p)
            there = link if there is None else there
            return pltpu.make_async_remote_copy(
                src_ref=ref, dst_ref=ref, send_sem=self.send.at[link, slot, p],
                recv_sem=self.recv.at[there, slot, p], device_id={"blk": target[link]}, device_id_type=MESH,
            )

        def sib_copy(self, index, link, slot, p):
            ref = self.part(index, p)
            return pltpu.make_async_remote_copy(
                src_ref=ref, dst_ref=ref, send_sem=self.sib_send.at[link, slot, p],
                recv_sem=self.sib_recv.at[link, slot, p], device_id={"blk": sibling}, device_id_type=MESH,
            )

        def both(self, body):
            for kind in (0, 1):
                pl.when(plane == kind)(functools.partial(body, kind))

        def send_slot(self, kind, slot, p):
            for link in range(LINKS):
                entry = _sent(kind, link, slot)
                if entry is not None:
                    self.link_copy(entry, link, slot, p, _received(kind, link)).start()

        def begin(self):
            @self.each
            def _(p):
                self.both(lambda kind: self.send_slot(kind, 0, p))
                self.sib_copy(me, LINKS, 0, p).start()

        def step(self, slot, p):
            def body(kind):
                for link, entries in ARRIVE[kind].items():
                    if entries[slot] is not None:
                        self.link_copy(entries[slot], link, slot, p).wait_recv()
                if slot + 1 < SLOTS:
                    self.send_slot(kind, slot + 1, p)
                for link, entries in ARRIVE[kind].items():
                    if entries[slot] is not None:
                        self.sib_copy(device(*entries[slot], core), link, slot, p).start()

            self.both(body)

        def unit(self, slot, n):
            link = n % LINKS
            code = jnp.int32(-1)
            for at in range(LINKS):
                ends = [ARRIVE[kind].get(at, [None] * SLOTS)[slot] for kind in (0, 1)]
                ends = [-1 if e is None else e[0] + 4 * e[1] for e in ends]
                code = jnp.where(link == at, jnp.where(middle, ends[1], ends[0]), code)
            from_core = core + (n // LINKS) * (1 - 2 * core)
            some = jnp.maximum(code, 0)
            return code >= 0, device(some % 4, some // 4, from_core), link

        def wait_sibling(self, index, link, slot):
            @self.each
            def _(p):
                self.sib_copy(index, link, slot, p).wait_recv()

        def drain(self):
            @self.each
            def _(p):
                def body(kind):
                    for slot in range(SLOTS):
                        for link in range(LINKS):
                            entry = _sent(kind, link, slot)
                            if entry is not None:
                                self.link_copy(entry, link, slot, p).wait_send()
                        for link, entries in ARRIVE[kind].items():
                            if entries[slot] is not None:
                                self.sib_copy(device(*entries[slot], core), link, slot, p).wait_send()

                self.both(body)
                self.sib_copy(me, LINKS, 0, p).wait_send()

    first = Phase(all_in, ROWS_IN, send_in, recv_in, sib_send_in, sib_recv_in)
    second = Phase(all_out, ROWS_OUT, send_out, recv_out, sib_send_out, sib_recv_out)
    depth_in, depth_out = all_in.shape[1], all_out.shape[1]

    def act_copy(index):
        columns = pl.ds(pl.multiple_of(index * depth_in, 128), depth_in)
        return pltpu.make_async_copy(act.at[:, columns], act_v, act_sem)

    def add_in(index):
        high, low = _split(all_in[index])
        block = act_v[...]
        total_in[...] += _dot(block, high) + _dot(block, low)

    def add_out(index):
        high, low = _split(all_out[index])
        block = grads_v[:, pl.ds(pl.multiple_of(index * depth_out, 128), depth_out)]
        total_out[...] += _dot(block, high) + _dot(block, low)

    def unit_in(slot, n, between):
        valid, index, link = first.unit(slot, n)
        pl.when(valid)(lambda: act_copy(index).start())
        between()

        @pl.when(valid)
        def _():
            pl.when(n >= LINKS)(lambda: first.wait_sibling(index, link, slot))
            act_copy(index).wait()
            add_in(index)

    def unit_out(slot, n):
        valid, index, link = second.unit(slot, n)

        @pl.when(valid)
        def _():
            pl.when(n >= LINKS)(lambda: second.wait_sibling(index, link, slot))
            add_out(index)

    def query_copy(chunk, at):
        rows = pl.ds(chunk * QUERY_STEP, QUERY_STEP)
        return pltpu.make_async_copy(query.at[rows], query_v.at[at], query_sem.at[at])

    own[1].wait()
    second.begin()
    own[2].wait()

    @pl.loop(0, UNITS)
    def _(n):
        second.at(n, lambda p: second.step(0, p))
        pl.when(n == 0)(lambda: add_out(me))

    second.wait_sibling(sibling, LINKS, 0)
    add_out(sibling)
    for slot in range(1, SLOTS):
        if slot == SLOTS - 1:
            own[0].wait()
            first.begin()

        @pl.loop(0, UNITS)
        def _(n, slot=slot):
            second.at(n, lambda p: second.step(slot, p))
            unit_out(slot - 1, n)

    query_copy(0, 0).start()

    @pl.loop(0, UNITS)
    def _(n):
        index = me + (n % 2) * (sibling - me)
        pl.when(n < 2)(lambda: act_copy(index).start())
        first.at(n, lambda p: first.step(0, p))

        @pl.when(n < 2)
        def _():
            pl.when(n == 1)(lambda: first.wait_sibling(sibling, LINKS, 0))
            act_copy(index).wait()
            add_in(index)

        @pl.when(n == 3)
        def _():
            @pl.loop(0, UNITS)
            def _(k):
                unit_out(SLOTS - 1, k)

            high, low = _split(total_out[...].T)
            r_high[...] = high
            r_low[...] = low

    chunks = query.shape[0] // QUERY_STEP

    def mix(chunk):
        at = chunk % 2
        pl.when(chunk + 1 < chunks)(lambda: query_copy(chunk + 1, 1 - at).start())
        query_copy(chunk, at).wait()
        for k in range(QUERY_STEP):
            scaled = (query_v[at, k].astype(F32) * inverse[...]).T
            s_high, s_low = _split(scaled)
            value = _dot(s_high, r_high[...]) + (_dot(s_high, r_low[...]) + _dot(s_low, r_high[...]))
            mixed[chunk * QUERY_STEP + k] = value

    def last_copy(n, index):
        source = pl.ds(pl.multiple_of(index * depth_in, 128), depth_in)
        columns = pl.ds(pl.multiple_of(n * depth_in, 128), depth_in)
        return pltpu.make_async_copy(act.at[:, source], grads_v.at[:, columns], last_sem.at[n])

    def add_piece(n, index, p):
        rows = first.length(p)
        high, low = _split(all_in[index, pl.ds(pl.multiple_of(p * first.rows, 128), rows)])
        block = grads_v[:, pl.ds(pl.multiple_of(n * depth_in + p * first.rows, 128), rows)]
        total_in[...] += _dot(block, high) + _dot(block, low)

    last = SLOTS - 1

    @pl.loop(0, UNITS)
    def _(n):
        valid, index, _ = first.unit(last, n)
        pl.when(valid)(lambda: last_copy(n, index).start())

    per_mix = pl.cdiv(chunks, (SLOTS - 2) * UNITS)
    for slot in range(1, SLOTS - 1):

        @pl.loop(0, UNITS)
        def _(n, slot=slot):
            unit_in(slot - 1, n, lambda: first.at(n, lambda p: first.step(slot, p)))
            for k in range(per_mix):
                chunk = ((slot - 1) * UNITS + n) * per_mix + k
                pl.when(chunk < chunks)(functools.partial(mix, chunk))

    @pl.loop(0, UNITS)
    def _(n):
        valid, index, _ = first.unit(last, n)
        pl.when(valid)(lambda: last_copy(n, index).wait())

    def pieces_of(base, p):
        @pl.loop(0, LINKS)
        def _(link):
            valid, index, _ = first.unit(last, base + link)

            @pl.when(valid)
            def _():
                if base:
                    first.sib_copy(index, link, last, p).wait_recv()
                add_piece(base + link, index, p)

    @pl.loop(0, UNITS)
    def _(n):
        unit_in(last - 1, n, lambda: first.at(n, lambda p: first.step(last, p)))
        first.at(n, lambda p: pieces_of(0, p))
        first.at(n, lambda p: pieces_of(LINKS, p), lag=1)

    turned = total_in[...].T

    @pl.loop(0, query.shape[0] // 8)
    def _(b):
        rows = pl.ds(pl.multiple_of(b * 8, 8), 8)
        scores[rows, :] = jnp.sum(mixed[rows] * turned[None], axis=1)

    first.drain()
    second.drain()


def gathered(activations, out_grads, input_basis, output_basis, query_rotated, eigenvalues):
    blocks = lax.axis_size("blk")
    tokens = activations.shape[0]
    queries, keep_out, keep_in = query_rotated.shape
    any_space = pl.BlockSpec(memory_space=pl.ANY)
    vmem = pl.BlockSpec(memory_space=pltpu.VMEM)

    def sems(pieces):
        dma = pltpu.SemaphoreType.DMA
        return [
            dma((LINKS, SLOTS, pieces)),
            dma((LINKS, SLOTS, pieces)),
            dma((LINKS + 1, SLOTS, pieces)),
            dma((LINKS + 1, SLOTS, pieces)),
        ]

    macs = tokens * (activations.shape[1] * keep_in + out_grads.shape[1] * keep_out)
    macs += tokens * queries * keep_out * keep_in
    return pl.pallas_call(
        kernel,
        out_shape=jax.ShapeDtypeStruct((queries, tokens), F32),
        in_specs=[any_space] * 5 + [vmem],
        out_specs=vmem,
        scratch_shapes=[
            pltpu.VMEM((blocks, *input_basis.shape), F32),
            pltpu.VMEM((blocks, *output_basis.shape), F32),
            pltpu.VMEM((queries, keep_in, tokens), F32),
            pltpu.VMEM(out_grads.shape, BF16),
            pltpu.VMEM((tokens, input_basis.shape[0]), BF16),
            pltpu.VMEM((2, QUERY_STEP, keep_out, keep_in), BF16),
            pltpu.VMEM((keep_out, keep_in), F32),
            pltpu.VMEM((tokens, keep_in), F32),
            pltpu.VMEM((tokens, keep_out), F32),
            pltpu.VMEM((keep_out, tokens), BF16),
            pltpu.VMEM((keep_out, tokens), BF16),
            *sems(pl.cdiv(input_basis.shape[0], ROWS_IN)),
            *sems(pl.cdiv(output_basis.shape[0], ROWS_OUT)),
            pltpu.SemaphoreType.DMA((3,)),
            pltpu.SemaphoreType.DMA,
            pltpu.SemaphoreType.DMA((2,)),
            pltpu.SemaphoreType.DMA((2 * LINKS,)),
        ],
        cost_estimate=pl.CostEstimate(flops=2 * macs, bytes_accessed=1 << 25, transcendentals=0),
        compiler_params=pltpu.CompilerParams(
            collective_id=0, has_side_effects=True, vmem_limit_bytes=63 << 20
        ),
    )(activations, out_grads, input_basis, output_basis, query_rotated, eigenvalues)


def per_device(activations, out_grads, input_basis, output_basis, query_rotated, eigenvalues):
    highest = lax.Precision.HIGHEST
    block = out_grads.astype(jnp.float32)
    out_part = jnp.dot(
        block,
        lax.all_gather(output_basis, "blk", axis=0, tiled=True),
        precision=highest,
        preferred_element_type=jnp.float32,
    )
    block = activations.astype(jnp.float32)
    in_part = jnp.dot(
        block,
        lax.all_gather(input_basis, "blk", axis=0, tiled=True),
        precision=highest,
        preferred_element_type=jnp.float32,
    )
    rotated_in = lax.psum_scatter(in_part, "col", scatter_dimension=1, tiled=True)
    rotated_out = lax.psum(out_part, "col")
    scaled = query_rotated.astype(jnp.float32) / eigenvalues[None, :, :]
    mixed = jnp.einsum(
        "qij,tj->qit", scaled, rotated_in, precision=highest, preferred_element_type=jnp.float32
    )
    partial_scores = jnp.einsum(
        "qit,ti->qt", mixed, rotated_out, precision=highest, preferred_element_type=jnp.float32
    )
    return lax.psum(partial_scores, "col")


def solution(mesh):
    shape = dict(mesh.shape)
    routed = shape["blk"] == 32 and shape["parts"] == 1 and shape["col"] == 1
    return jax.shard_map(
        gathered if routed else per_device,
        mesh=mesh,
        in_specs=(
            P(("parts", "blk"), "col"),
            P(("parts", "blk"), "col"),
            P(("parts", "col", "blk"), None),
            P(("parts", "col", "blk"), None),
            P("parts", None, "col"),
            P("parts", "col"),
        ),
        out_specs=P("parts", "blk"),
        check_vma=False,
    )
```
